512 devices in a mesh: node: 128 (over z, x, y_lo), rep: 4 (over y_hi, core).
Axes of the slice: x: 4, y: 4 (y_hi: 2, y_lo: 2; y = y_hi * 2 + y_lo), z: 16, core: 2. Of those that a mesh axis runs over, the one named last changes fastest.
Arguments:
- features: bfloat16 [16384, 256], P('node'), may hold values from -6 to 6
- weight: bfloat16 [256, 256], replicated, may hold values from -0.375 to 0.375
- out_grad: bfloat16 [16384, 256], P('node'), may hold values from -6 to 6
- tile_place: int32 [128, 4, 32], P('node', 'rep'), may hold values from 0 to 32, as said below
- tile_bits: int32 [128, 4, 32, 16, 128], P('node', 'rep'), may hold values from 0 to 255, as said below
- back_place: int32 [128, 4, 32], P('node', 'rep'), may hold values from 0 to 32, as said below
- back_bits: int32 [128, 4, 32, 16, 128], P('node', 'rep'), may hold values from 0 to 255, as said below
Outputs:
- activation: bfloat16 [16384, 256], P('node')
- weight_grad: float32 [256, 256], replicated
- input_grad: bfloat16 [16384, 256], P('node')
The draws below stay inside these ranges and needn't reach their ends.
Inputs may be any that keep to these rules, and one draw needn't show every extreme that they name: `tile_place`: in each shard the positions of its nonzero tiles stand first in ascending order, then every remaining slot holds 32; the shard of node index 0 and rep index 0 has all 32 tiles nonzero. `tile_bits`: slots holding 32 in tile_place have all words 0. `back_place`: as tile_place, for the transposed adjacency; the shard of node index 0 and rep index 0 is full. `back_bits`: slots holding 32 in back_place have all words 0; the tiles are the transposes of those of tile_bits.
All inputs are finite; a program needn't handle non-finite values.
Results may differ from the reference program's by a relative error of at most 0.0058.
Values may be sent and summed in bfloat16 or wider, within the bound.
No kernel may reach another device: no remote copies, remote signals or barrier semaphores. Data moves between devices by JAX's collectives and lax.ppermute only.
A program may use at most 64 MiB of HBM per device.

```python
import jax
import jax.numpy as jnp
from jax import lax

F = 256
HID = 256
ROWS = 128
SLOTS = 32
NODES = 16384
N_NODE = 128
N_REP = 4


def tile_world(key):
    block_count = N_NODE
    tile_count = ROWS // 128
    first, second, third, fourth = jax.random.split(key, 4)
    row_level = jax.random.randint(first, (block_count,), 30, 101)
    col_level = jax.random.randint(second, (block_count,), 30, 101)
    rolled = jax.random.randint(third, (block_count, block_count, tile_count, tile_count), 0, 10000)
    present = rolled < (row_level[:, None] * col_level[None, :])[:, :, None, None]
    index_line = jnp.arange(block_count)
    forced = (index_line[:, None] == 0) & (index_line[None, :] % N_REP == 0) | (index_line[None, :] == 0) & (index_line[:, None] % N_REP == 0)
    present = present | forced[:, :, None, None]
    packed = jax.random.randint(fourth, (block_count, block_count, tile_count, tile_count, 16, 128), 0, 256)
    packed = jnp.where(present[..., None, None], packed, 0)
    return (present, packed)


def arrange(present, packed):
    block_count = N_NODE
    tile_count = ROWS // 128
    section_total = block_count // N_REP
    live = present.reshape(block_count, section_total, N_REP, tile_count, tile_count).transpose(0, 2, 1, 3, 4).reshape(block_count, N_REP, SLOTS)
    tiles_all = packed.reshape(block_count, section_total, N_REP, tile_count, tile_count, 16, 128).transpose(0, 2, 1, 3, 4, 5, 6).reshape(block_count, N_REP, SLOTS, 16, 128)
    position = jnp.arange(SLOTS, dtype=jnp.int32)
    order_key = jnp.where(live, position, SLOTS + position)
    ordering = jnp.argsort(order_key, axis=-1)
    sorted_key = jnp.take_along_axis(order_key, ordering, axis=-1)
    positions = jnp.where(sorted_key < SLOTS, sorted_key, SLOTS).astype(jnp.int32)
    sorted_bits = jnp.take_along_axis(tiles_all, ordering[..., None, None], axis=2)
    return (positions, sorted_bits.astype(jnp.int32))


def flip_tiles(packed):
    shifts = jnp.arange(8, dtype=jnp.int32)

    def one_block(row_words):
        pattern = jnp.bitwise_and(jnp.right_shift(row_words[..., :, None, :], shifts[:, None]), 1)
        square = pattern.reshape(row_words.shape[:-2] + (128, 128))
        turned = jnp.swapaxes(square, -1, -2).reshape(row_words.shape[:-2] + (16, 8, 128))
        return jnp.sum(jnp.left_shift(turned, shifts[:, None]), axis=-2)
    return lax.map(one_block, packed)


def transposed_lists(key):
    present, packed = tile_world(key)
    flipped = flip_tiles(packed)
    return arrange(present.transpose(1, 0, 3, 2), flipped.transpose(1, 0, 3, 2, 4, 5))


def draw_tile_place(key, part):
    present, packed = tile_world(key)
    return arrange(present, packed)[0]


def draw_tile_bits(key, part):
    present, packed = tile_world(key)
    return arrange(present, packed)[1]


def draw_back_place(key, part):
    result = transposed_lists(key)
    return result[0]


def draw_back_bits(key, part):
    result = transposed_lists(key)
    return result[1]


def block_scale(own_key, dims, cuts, smallest, high):
    def one(dim, shards_of):
        steps = jax.random.uniform(jax.random.fold_in(jax.random.fold_in(own_key, 6), dim), (shards_of,), jnp.float32, smallest / len(cuts), high / len(cuts))
        return jnp.repeat(jnp.exp(steps), dims[dim] // shards_of).reshape((-1,) + (1,) * (len(dims) - dim - 1))

    loudness = one(*cuts[0])
    for cut in cuts[1:]:
        loudness = loudness * one(*cut)
    return loudness


def normal_values(own_key, extent, width, reach, cuts=(), held_as=jnp.bfloat16):
    values = width * jax.random.normal(own_key, extent, jnp.float32)
    if cuts:
        values = values * block_scale(own_key, extent, cuts, -0.22, 0.18)
    return jnp.clip(values, -reach, reach).astype(held_as)


def setup_inputs(seed: int = 0) -> dict:
    key_of = jax.random.split(jax.random.key(seed), 8)
    return {
        "features": normal_values(key_of[0], (NODES, F), 1.0, 6.0, ((0, 128),)),
        "weight": normal_values(key_of[1], (F, HID), F ** -0.5, 0.375),
        "out_grad": normal_values(key_of[2], (NODES, HID), 1.0, 6.0, ((0, 128),)),
        "tile_place": draw_tile_place(jax.random.fold_in(key_of[7], 71), 0),
        "tile_bits": draw_tile_bits(jax.random.fold_in(key_of[7], 71), 0),
        "back_place": draw_back_place(jax.random.fold_in(key_of[7], 71), 0),
        "back_bits": draw_back_bits(jax.random.fold_in(key_of[7], 71), 0),
    }


def unpack(packed):
    shifts = jnp.arange(8, dtype=jnp.int32)
    pattern = jnp.bitwise_and(jnp.right_shift(packed[..., :, None, :], shifts[:, None]), 1)
    return pattern.reshape(packed.shape[:-2] + (128, 128))

def aggregate(place_all, bits_all, source):
    tile_count = ROWS // 128
    per_section = tile_count * tile_count
    section_total = N_NODE // N_REP
    feature_width = source.shape[1]
    source_tiles = source.reshape(-1, 128, feature_width)
    flat_place = place_all.reshape(N_NODE * N_REP, -1)
    flat_bits = bits_all.reshape((N_NODE * N_REP,) + bits_all.shape[2:])

    def one_device(item):
        device, positions, packed = item
        rep_index = device % N_REP
        current = jnp.minimum(positions // per_section, section_total - 1)
        position = positions % per_section
        row_tile = position // tile_count
        col_tile = (current * N_REP + rep_index) * tile_count + position % tile_count
        pattern = unpack(packed).astype(jnp.float32)
        operand = source_tiles[col_tile].astype(jnp.float32)
        product = jnp.einsum('svu,svf->suf', pattern, operand)
        choose = (row_tile[:, None] == jnp.arange(tile_count, dtype=jnp.int32)[None, :]).astype(jnp.float32)
        running = jnp.einsum('sa,suf->auf', choose, product).reshape(ROWS, feature_width)
        degree = jnp.einsum('sa,su->au', choose, lax.optimization_barrier(jnp.sum(pattern, axis=1))).reshape(ROWS)
        return (running, degree)
    devices = jnp.arange(N_NODE * N_REP, dtype=jnp.int32)
    totals, degrees = lax.map(one_device, (devices, flat_place, flat_bits))
    totals = totals.reshape(N_NODE, N_REP, ROWS, feature_width).sum(axis=1).reshape(-1, feature_width)
    degrees = degrees.reshape(N_NODE, N_REP, ROWS).sum(axis=1).reshape(-1)
    return (totals, degrees)

def reference(features, weight, out_grad, tile_place, tile_bits, back_place, back_bits):
    gathered, counted = aggregate(tile_place, tile_bits, features)
    scaling = lax.rsqrt(1.0 + counted)[:, None]
    hidden = (features.astype(jnp.float32) + gathered * scaling).astype(jnp.bfloat16)
    logits = jnp.dot(hidden, weight, preferred_element_type=jnp.float32)
    sigmoid_part = jax.nn.sigmoid(logits)
    activation = (logits * sigmoid_part).astype(jnp.bfloat16)
    upstream = (out_grad.astype(jnp.float32) * sigmoid_part * (1.0 + logits * (1.0 - sigmoid_part))).astype(jnp.bfloat16)
    weight_grad = jnp.dot(hidden.T, upstream, preferred_element_type=jnp.float32)
    hidden_grad = jnp.dot(upstream, weight.T, preferred_element_type=jnp.float32)
    pushed = (hidden_grad * scaling).astype(jnp.bfloat16)
    back_total, unused = aggregate(back_place, back_bits, pushed)
    input_grad = (hidden_grad + back_total).astype(jnp.bfloat16)
    return (activation, weight_grad, input_grad)
```

```python
import jax
import jax.numpy as jnp
from jax import lax
from jax.experimental import pallas as pl
from jax.experimental.pallas import tpu as pltpu
from jax.sharding import Mesh, PartitionSpec as P

BF, F32, I32 = jnp.bfloat16, jnp.float32, jnp.int32
NODE, REP = ("z", "x", "yl"), ("yh", "c")
ROWS2, PLANE = ("x", "yl"), ("x", "yl", "yh", "c")
Z, K8, R4, PL = 16, 8, 4, 32
Q, W = 32, 256
PARAMS = pltpu.CompilerParams(vmem_limit_bytes=24 * 1024 * 1024)


def where_am_i():
    x = lax.axis_index("x")
    q = (x % 2) * 2 + lax.axis_index("yl")
    return x // 2, q, lax.axis_index("yh") * 2 + lax.axis_index("c")


def swap_pairs():
    pairs = []
    for x1 in range(2):
        for a in range(4):
            for b in range(4):
                pairs.append((x1 * 16 + a * 4 + b, x1 * 16 + b * 4 + a))
    return pairs


def call(body, shapes, *args):
    return pl.pallas_call(
        body,
        out_shape=shapes,
        in_specs=[pl.BlockSpec(memory_space=pltpu.VMEM)] * len(args),
        out_specs=jax.tree.map(lambda _: pl.BlockSpec(memory_space=pltpu.VMEM), shapes),
        compiler_params=PARAMS,
    )(*args)


def words_body(place_f, bits_f, place_b, bits_b, out):
    row = lax.broadcasted_iota(I32, (512, 512), 0)
    want = (((row // 4) % 16) * 2 + row // 256) * 16 + ((row // 64) % 4) * 4 + row % 4
    lane = lax.broadcasted_iota(I32, (32, 512), 1)
    spread = jnp.where(lane // 16 == lax.broadcasted_iota(I32, (32, 512), 0), 1.0, 0.0).astype(BF)
    column = lax.broadcasted_iota(I32, (8, 512), 1) % 16
    for half, (place, bits) in enumerate(((place_f, bits_f), (place_b, bits_b))):
        at = jnp.broadcast_to(place[...].astype(F32), (8, 32)).astype(BF)
        key = jnp.dot(at, spread, preferred_element_type=F32).astype(I32) * 16 + column
        hot = jnp.where(want == key[0:1, :], 1.0, 0.0).astype(BF)
        dense = jnp.dot(hot, bits[...].astype(F32).astype(BF), preferred_element_type=F32).astype(BF)
        for k in range(K8):
            out[k, half * 64 : half * 64 + 64, :] = dense[k * 64 : (k + 1) * 64]


def unpacked(words):
    spread = jnp.broadcast_to(words.astype(F32).astype(I32)[:, None, :], (64, 8, 128))
    bits = jnp.bitwise_and(jnp.right_shift(spread, lax.broadcasted_iota(I32, (64, 8, 128), 1)), 1)
    return bits.reshape(512, 128).astype(F32).astype(BF)


def over_columns(block, source):
    return lax.dot_general(block, source, (((0,), (0,)), ((), ())), preferred_element_type=F32)


def forward_body(words, gathered, out):
    source = gathered[...].reshape(Z * Q, W)
    upper = lax.broadcasted_iota(I32, (16, 512), 1) // 256
    ones = jnp.where(upper == lax.broadcasted_iota(I32, (16, 512), 0), 1.0, 0.0).astype(BF)
    for k in range(K8):
        block = unpacked(words[k, 0:64, :])
        part = over_columns(block, source).astype(BF)
        degree = jnp.dot(ones, block, preferred_element_type=F32).astype(BF)
        for q in range(4):
            dest = (k // 4) * 16 + q * 4 + k % 4
            out[dest, 0:32, :] = part[q * 32 : (q + 1) * 32]
            out[dest, 32:48, 0:128] = degree
            out[dest, 32:48, 128:256] = jnp.zeros_like(degree)


def middle_body(parts, own, weight, act, back, pushed, term):
    total = jnp.sum(parts[...].astype(F32), axis=0)
    x1, q, r = where_am_i()
    degree = total[32:33, 0:128] + total[33:34, 0:128]
    pick = lax.broadcasted_iota(I32, (32, 128), 1) == lax.broadcasted_iota(I32, (32, 128), 0) + q * 32
    counted = jnp.sum(jnp.where(pick, degree, 0.0), axis=1, keepdims=True)
    scaling = lax.rsqrt(1.0 + counted)
    hidden = (own[0:32, :].astype(F32) + total[0:32] * scaling).astype(BF)
    logits = jnp.dot(hidden, weight[...], preferred_element_type=F32)
    gate = jax.nn.sigmoid(logits)
    act[...] = (logits * gate).astype(BF)
    upstream = (own[32:64, :].astype(F32) * gate * (1.0 + logits * (1.0 - gate))).astype(BF)
    hidden_grad = lax.dot_general(
        upstream, weight[...], (((1,), (1,)), ((), ())), preferred_element_type=F32
    )
    back[...] = hidden_grad
    pushed[...] = (hidden_grad * scaling).astype(BF)
    term[...] = over_columns(hidden, upstream).astype(BF)


def two_parts(value):
    high = value.astype(BF).astype(F32)
    return jnp.concatenate([high, value - high], axis=0).astype(BF)


def send_body(terms, pushed, out):
    extra = two_parts(jnp.sum(terms[...].astype(F32), axis=0))
    for z in range(Z):
        out[z, 0:32, :] = pushed[...]
        out[z, 32:48, :] = extra


def backward_body(words, gathered, hidden_grad, out):
    x1, q, r = where_am_i()
    mine = (x1 * 4 + r) * 4 + q
    source = gathered[:, 0:32, :].reshape(Z * Q, W)
    slices = jnp.sum(gathered[:, 32:48, :].astype(F32), axis=0)
    extra = two_parts(slices[0:8] + slices[8:16])
    own = hidden_grad[...]
    for k in range(K8):
        part = over_columns(unpacked(words[k, 64:128, :]), source)
        for t in range(4):
            dest = k * 4 + t
            piece = part[t * 32 : (t + 1) * 32] + jnp.where(mine == dest, own, 0.0)
            out[dest, 0:32, :] = piece.astype(BF)
            out[dest, 32:48, :] = extra


def per_device(features, weight, out_grad, tile_place, tile_bits, back_place, back_bits):
    x1, q, r = where_am_i()
    quarter = jnp.concatenate(
        [lax.dynamic_slice_in_dim(a, r * Q, Q, 0) for a in (features, out_grad)], axis=0
    )
    own = lax.ppermute(quarter, PLANE, swap_pairs())
    words = call(
        words_body,
        jax.ShapeDtypeStruct((K8, 128, 128), BF),
        tile_place.reshape(1, 32),
        tile_bits.reshape(512, 128),
        back_place.reshape(1, 32),
        back_bits.reshape(512, 128),
    )
    words = lax.all_to_all(words, ROWS2, 0, 0)
    gathered = lax.all_to_all(jnp.broadcast_to(own[None, :Q], (Z, Q, W)), "z", 0, 0)
    parts = call(forward_body, jax.ShapeDtypeStruct((PL, 48, W), BF), words, gathered)
    parts = lax.all_to_all(parts, PLANE, 0, 0)
    act, hidden_grad, pushed, term = call(
        middle_body,
        (
            jax.ShapeDtypeStruct((Q, W), BF),
            jax.ShapeDtypeStruct((Q, W), F32),
            jax.ShapeDtypeStruct((Q, W), BF),
            jax.ShapeDtypeStruct((W, W), BF),
        ),
        parts,
        own,
        weight,
    )
    act = lax.ppermute(act, PLANE, swap_pairs())
    terms = lax.all_to_all(term.reshape(PL, 8, W), PLANE, 0, 0)
    sent = call(send_body, jax.ShapeDtypeStruct((Z, 48, W), BF), terms, pushed)
    gathered = lax.all_to_all(sent, "z", 0, 0)
    parts = call(
        backward_body, jax.ShapeDtypeStruct((PL, 48, W), BF), words, gathered, hidden_grad
    )
    parts = lax.all_to_all(parts, PLANE, 0, 0)
    input_grad = jnp.sum(parts[:, 0:32].astype(F32), axis=0).astype(BF)
    slices = parts[:, 32:48].astype(F32)
    weight_grad = (slices[:, 0:8] + slices[:, 8:16]).reshape(W, W)
    both = lax.all_gather(jnp.concatenate([act, input_grad], axis=0), REP, axis=0)
    return both[:, :Q].reshape(4 * Q, W), weight_grad, both[:, Q:].reshape(4 * Q, W)


def solution(mesh):
    fine = Mesh(mesh.devices.reshape(16, 4, 2, 2, 2), ("z", "x", "yl", "yh", "c"))
    return jax.shard_map(
        per_device,
        mesh=fine,
        in_specs=(
            P(NODE, None),
            P(),
            P(NODE, None),
            P(NODE, REP, None),
            P(NODE, REP, None, None, None),
            P(NODE, REP, None),
            P(NODE, REP, None, None, None),
        ),
        out_specs=(P(NODE, None), P(), P(NODE, None)),
        check_vma=False,
    )
```

```python
import jax
import jax.numpy as jnp
from jax import lax
from jax.experimental import pallas as pl
from jax.experimental.pallas import tpu as pltpu
from jax.sharding import Mesh, PartitionSpec as P

BF, F32, I32 = jnp.bfloat16, jnp.float32, jnp.int32
NODE, REP = ("z", "x", "yl"), ("yh", "c")
ROWS2, PLANE = ("x", "yl"), ("x", "yl", "yh", "c")
Z, K8, R4, PL = 16, 8, 4, 32
Q, W = 32, 256
PARAMS = pltpu.CompilerParams(vmem_limit_bytes=24 * 1024 * 1024)


def where_am_i():
    x = lax.axis_index("x")
    q = (x % 2) * 2 + lax.axis_index("yl")
    return x // 2, q, lax.axis_index("yh") * 2 + lax.axis_index("c")


def swap_pairs():
    pairs = []
    for x1 in range(2):
        for a in range(4):
            for b in range(4):
                pairs.append((x1 * 16 + a * 4 + b, x1 * 16 + b * 4 + a))
    return pairs


def call(body, shapes, *args):
    return pl.pallas_call(
        body,
        out_shape=shapes,
        in_specs=[pl.BlockSpec(memory_space=pltpu.VMEM)] * len(args),
        out_specs=jax.tree.map(lambda _: pl.BlockSpec(memory_space=pltpu.VMEM), shapes),
        compiler_params=PARAMS,
    )(*args)


def words_body(place, bits, features, out):
    row = lax.broadcasted_iota(I32, (512, 512), 0)
    want = (((row // 4) % 16) * 2 + row // 256) * 16 + ((row // 64) % 4) * 4 + row % 4
    lane = lax.broadcasted_iota(I32, (32, 512), 1)
    spread = jnp.where(lane // 16 == lax.broadcasted_iota(I32, (32, 512), 0), 1.0, 0.0).astype(BF)
    column = lax.broadcasted_iota(I32, (8, 512), 1) % 16
    at = jnp.broadcast_to(place[...].astype(F32), (8, 32)).astype(BF)
    key = jnp.dot(at, spread, preferred_element_type=F32).astype(I32) * 16 + column
    hot = jnp.where(want == key[0:1, :], 1.0, 0.0).astype(BF)
    dense = jnp.dot(hot, bits[...].astype(F32).astype(BF), preferred_element_type=F32).astype(BF)
    for k in range(K8):
        out[k, 0:32, 0:128] = dense[k * 64 : k * 64 + 32]
        out[k, 0:32, 128:256] = dense[k * 64 + 32 : k * 64 + 64]
        out[k, 32:160, :] = features[...]


def unpacked(words):
    halves = []
    for h in range(2):
        half = words[:, h * 128 : (h + 1) * 128].astype(F32).astype(I32)
        spread = jnp.broadcast_to(half[:, None, :], (32, 8, 128))
        bits = jnp.bitwise_and(jnp.right_shift(spread, lax.broadcasted_iota(I32, (32, 8, 128), 1)), 1)
        halves.append(bits.reshape(256, 128).astype(F32).astype(BF))
    return jnp.concatenate(halves, axis=0)


def over_rows(block, source):
    return lax.dot_general(block, source, (((0,), (0,)), ((), ())), preferred_element_type=F32)


def forward_body(plane, out):
    block = jnp.concatenate([unpacked(plane[k, 0:32, :]) for k in range(K8)], axis=1)
    source = plane[:, 32:160, :].reshape(K8 * 128, W)
    part = jnp.dot(block, source, preferred_element_type=F32)
    fourth = lax.broadcasted_iota(I32, (16, 1024), 1) // 256
    ones = jnp.where(fourth == lax.broadcasted_iota(I32, (16, 1024), 0), 1.0, 0.0).astype(BF)
    degree = lax.dot_general(ones, block, (((1,), (1,)), ((), ())), preferred_element_type=F32)
    for z in range(Z):
        lanes = degree[0:8, (z // 4) * 128 : (z // 4 + 1) * 128]
        tail = jnp.concatenate([lanes, jnp.zeros_like(lanes)], axis=1)
        out[z] = jnp.concatenate([part[z * 32 : (z + 1) * 32], tail], axis=0).astype(BF)


def middle_body(parts, own, weight, act, back, pushed, term):
    total = jnp.sum(parts[...].astype(F32), axis=0)
    degree = jnp.sum(total[32:36, 0:128], axis=0, keepdims=True)
    first = (lax.axis_index("z") % 4) * 32
    pick = lax.broadcasted_iota(I32, (32, 128), 1) == lax.broadcasted_iota(I32, (32, 128), 0) + first
    counted = jnp.sum(jnp.where(pick, degree, 0.0), axis=1, keepdims=True)
    scaling = lax.rsqrt(1.0 + counted)
    hidden = (own[0:32, :].astype(F32) + total[0:32] * scaling).astype(BF)
    logits = jnp.dot(hidden, weight[...], preferred_element_type=F32)
    gate = jax.nn.sigmoid(logits)
    act[...] = (logits * gate).astype(BF)
    upstream = (own[32:64, :].astype(F32) * gate * (1.0 + logits * (1.0 - gate))).astype(BF)
    hidden_grad = lax.dot_general(
        upstream, weight[...], (((1,), (1,)), ((), ())), preferred_element_type=F32
    )
    back[...] = hidden_grad
    pushed[...] = (hidden_grad * scaling).astype(BF)
    term[...] = over_rows(hidden, upstream).astype(BF)


def two_parts(value):
    high = value.astype(BF).astype(F32)
    return jnp.concatenate([high, value - high], axis=0).astype(BF)


def send_body(terms, pushed, out):
    extra = jnp.sum(terms[...].astype(F32), axis=0)
    message = jnp.concatenate([pushed[...].astype(F32), extra], axis=0).astype(BF)
    for z in range(Z):
        out[z] = message


def backward_body(plane, gathered, hidden_grad, out):
    x1, q, r = where_am_i()
    mine = (x1 * 4 + r) * 4 + q
    received = gathered[...].astype(F32)
    source = received[:, 0:32].reshape(Z * Q, W).astype(BF)
    extra = two_parts(jnp.sum(received[:, 32:40], axis=0))
    own = hidden_grad[...]
    for k in range(K8):
        part = over_rows(unpacked(plane[k, 0:32, :]), source)
        for t in range(4):
            dest = k * 4 + t
            piece = part[t * 32 : (t + 1) * 32] + jnp.where(mine == dest, own, 0.0)
            out[dest, 0:32, :] = piece.astype(BF)
            out[dest, 32:48, :] = extra


def per_device(features, weight, out_grad, tile_place, tile_bits, back_place, back_bits):
    x1, q, r = where_am_i()
    quarter = jnp.concatenate(
        [lax.dynamic_slice_in_dim(a, r * Q, Q, 0) for a in (features, out_grad)], axis=0
    )
    own = lax.ppermute(quarter, PLANE, swap_pairs())
    plane = call(
        words_body,
        jax.ShapeDtypeStruct((K8, 160, W), BF),
        back_place.reshape(1, 32),
        back_bits.reshape(512, 128),
        features,
    )
    plane = lax.all_to_all(plane, ROWS2, 0, 0)
    parts = call(forward_body, jax.ShapeDtypeStruct((Z, 40, W), BF), plane)
    parts = lax.all_to_all(parts, "z", 0, 0)
    act, hidden_grad, pushed, term = call(
        middle_body,
        (
            jax.ShapeDtypeStruct((Q, W), BF),
            jax.ShapeDtypeStruct((Q, W), F32),
            jax.ShapeDtypeStruct((Q, W), BF),
            jax.ShapeDtypeStruct((W, W), BF),
        ),
        parts,
        own,
        weight,
    )
    act = lax.ppermute(act, PLANE, swap_pairs())
    terms = lax.all_to_all(term.reshape(PL, 8, W), PLANE, 0, 0)
    sent = call(send_body, jax.ShapeDtypeStruct((Z, 40, W), BF), terms, pushed)
    gathered = lax.all_to_all(sent, "z", 0, 0)
    parts = call(
        backward_body, jax.ShapeDtypeStruct((PL, 48, W), BF), plane, gathered, hidden_grad
    )
    parts = lax.all_to_all(parts, PLANE, 0, 0)
    input_grad = jnp.sum(parts[:, 0:32].astype(F32), axis=0).astype(BF)
    slices = parts[:, 32:48].astype(F32)
    weight_grad = (slices[:, 0:8] + slices[:, 8:16]).reshape(W, W)
    both = lax.all_gather(jnp.concatenate([act, input_grad], axis=0), REP, axis=0)
    return both[:, :Q].reshape(4 * Q, W), weight_grad, both[:, Q:].reshape(4 * Q, W)


def solution(mesh):
    fine = Mesh(mesh.devices.reshape(16, 4, 2, 2, 2), ("z", "x", "yl", "yh", "c"))
    return jax.shard_map(
        per_device,
        mesh=fine,
        in_specs=(
            P(NODE, None),
            P(),
            P(NODE, None),
            P(NODE, REP, None),
            P(NODE, REP, None, None, None),
            P(NODE, REP, None),
            P(NODE, REP, None, None, None),
        ),
        out_specs=(P(NODE, None), P(), P(NODE, None)),
        check_vma=False,
    )
```

```python
import jax
import jax.numpy as jnp
from jax import lax
from jax.experimental import pallas as pl
from jax.experimental.pallas import tpu as pltpu
from jax.sharding import Mesh, PartitionSpec as P

BF, F32, I32 = jnp.bfloat16, jnp.float32, jnp.int32
NODE, REP = ("z", "x", "yl"), ("yh", "c")
ROWS2, PLANE = ("x", "yl"), ("x", "yl", "yh", "c")
Z, K8, R4, PL = 16, 8, 4, 32
Q, W = 32, 256
PARAMS = pltpu.CompilerParams(vmem_limit_bytes=24 * 1024 * 1024)


def where_am_i():
    x = lax.axis_index("x")
    q = (x % 2) * 2 + lax.axis_index("yl")
    return x // 2, q, lax.axis_index("yh") * 2 + lax.axis_index("c")


def swap_pairs():
    pairs = []
    for x1 in range(2):
        for a in range(4):
            for b in range(4):
                pairs.append((x1 * 16 + a * 4 + b, x1 * 16 + b * 4 + a))
    return pairs


def call(body, shapes, *args):
    return pl.pallas_call(
        body,
        out_shape=shapes,
        in_specs=[pl.BlockSpec(memory_space=pltpu.VMEM)] * len(args),
        out_specs=jax.tree.map(lambda _: pl.BlockSpec(memory_space=pltpu.VMEM), shapes),
        compiler_params=PARAMS,
    )(*args)


def words_body(place, bits_far, features_far, out, bits, features, sems):
    fetches = [
        pltpu.make_async_copy(bits_far, bits, sems.at[0]),
        pltpu.make_async_copy(features_far, features, sems.at[1]),
    ]
    for fetch in fetches:
        fetch.start()
    row = lax.broadcasted_iota(I32, (512, 512), 0)
    want = (((row // 4) % 16) * 2 + row // 256) * 16 + ((row // 64) % 4) * 4 + row % 4
    lane = lax.broadcasted_iota(I32, (32, 512), 1)
    spread = jnp.where(lane // 16 == lax.broadcasted_iota(I32, (32, 512), 0), 1.0, 0.0).astype(BF)
    column = lax.broadcasted_iota(I32, (8, 512), 1) % 16
    at = jnp.broadcast_to(place[...].astype(F32), (8, 32)).astype(BF)
    key = jnp.dot(at, spread, preferred_element_type=F32).astype(I32) * 16 + column
    hot = jnp.where(want == key[0:1, :], 1.0, 0.0).astype(BF)
    for fetch in fetches:
        fetch.wait()
    dense = jnp.dot(hot, bits[...].astype(F32).astype(BF), preferred_element_type=F32).astype(BF)
    for k in range(K8):
        out[k, 0:32, 0:128] = dense[k * 64 : k * 64 + 32]
        out[k, 0:32, 128:256] = dense[k * 64 + 32 : k * 64 + 64]
        out[k, 32:160, :] = features[...]


def unpacked(words):
    halves = []
    for h in range(2):
        half = words[:, h * 128 : (h + 1) * 128].astype(F32).astype(I32)
        spread = jnp.broadcast_to(half[:, None, :], (32, 8, 128))
        bits = jnp.bitwise_and(jnp.right_shift(spread, lax.broadcasted_iota(I32, (32, 8, 128), 1)), 1)
        halves.append(bits.reshape(256, 128).astype(F32).astype(BF))
    return jnp.concatenate(halves, axis=0)


def over_rows(block, source):
    return lax.dot_general(block, source, (((0,), (0,)), ((), ())), preferred_element_type=F32)


def forward_body(plane, out):
    block = jnp.concatenate([unpacked(plane[k, 0:32, :]) for k in range(K8)], axis=1)
    source = plane[:, 32:160, :].reshape(K8 * 128, W)
    part = jnp.dot(block, source, preferred_element_type=F32)
    fourth = lax.broadcasted_iota(I32, (16, 1024), 1) // 256
    ones = jnp.where(fourth == lax.broadcasted_iota(I32, (16, 1024), 0), 1.0, 0.0).astype(BF)
    degree = lax.dot_general(ones, block, (((1,), (1,)), ((), ())), preferred_element_type=F32)
    for z in range(Z):
        lanes = degree[0:8, (z // 4) * 128 : (z // 4 + 1) * 128]
        tail = jnp.concatenate([lanes, jnp.zeros_like(lanes)], axis=1)
        out[z] = jnp.concatenate([part[z * 32 : (z + 1) * 32], tail], axis=0).astype(BF)


def middle_body(parts, own, weight, act, back, pushed, term):
    total = jnp.sum(parts[...].astype(F32), axis=0)
    degree = jnp.sum(total[32:36, 0:128], axis=0, keepdims=True)
    first = (lax.axis_index("z") % 4) * 32
    pick = lax.broadcasted_iota(I32, (32, 128), 1) == lax.broadcasted_iota(I32, (32, 128), 0) + first
    counted = jnp.sum(jnp.where(pick, degree, 0.0), axis=1, keepdims=True)
    scaling = lax.rsqrt(1.0 + counted)
    hidden = (own[0:32, :].astype(F32) + total[0:32] * scaling).astype(BF)
    logits = jnp.dot(hidden, weight[...], preferred_element_type=F32)
    gate = jax.nn.sigmoid(logits)
    act[...] = (logits * gate).astype(BF)
    upstream = (own[32:64, :].astype(F32) * gate * (1.0 + logits * (1.0 - gate))).astype(BF)
    hidden_grad = lax.dot_general(
        upstream, weight[...], (((1,), (1,)), ((), ())), preferred_element_type=F32
    )
    back[...] = hidden_grad
    pushed[...] = (hidden_grad * scaling).astype(BF)
    term[...] = over_rows(hidden, upstream).astype(BF)


def two_parts(value):
    high = value.astype(BF).astype(F32)
    return jnp.concatenate([high, value - high], axis=0).astype(BF)


def send_body(terms, pushed, out):
    extra = jnp.sum(terms[...].astype(F32), axis=0)
    message = jnp.concatenate([pushed[...].astype(F32), extra], axis=0).astype(BF)
    for z in range(Z):
        out[z] = message


def backward_body(plane, gathered, hidden_grad, out, total):
    x1, q, r = where_am_i()
    received = gathered[...].astype(F32)
    source = received[:, 0:32].reshape(Z * Q, W).astype(BF)
    extra = two_parts(jnp.sum(received[:, 32:40], axis=0))
    for k in range(K8):
        total[k] = over_rows(unpacked(plane[k, 0:32, :]), source)
    rows = pl.ds(pl.multiple_of(q * 32, 32), 32)
    total[x1 * 4 + r, rows, :] = total[x1 * 4 + r, rows, :] + hidden_grad[...]
    for k in range(K8):
        out[k, 0:128, :] = total[k].astype(BF)
        out[k, 128:144, :] = extra


def share_body(parts, act, out):
    out[0:128, :] = jnp.sum(parts[:, 0:128, :].astype(F32), axis=0).astype(BF)
    for k in range(K8):
        out[128 + k * 16 : 144 + k * 16, :] = parts[k, 128:144, :]
    out[256:288, :] = act[...]


def finish_body(shares, activation, weight_grad, input_grad):
    input_grad[...] = jnp.sum(shares[:, 0:128, :].astype(F32), axis=0).astype(BF)
    for r in range(R4):
        activation[r * 32 : (r + 1) * 32, :] = shares[r, 256:288, :]
        for k in range(K8):
            both = shares[r, 128 + k * 16 : 144 + k * 16, :].astype(F32)
            weight_grad[k * 32 + r * 8 : k * 32 + r * 8 + 8, :] = both[0:8] + both[8:16]


def per_device(features, weight, out_grad, tile_place, tile_bits, back_place, back_bits):
    x1, q, r = where_am_i()
    quarter = jnp.concatenate(
        [lax.dynamic_slice_in_dim(a, r * Q, Q, 0) for a in (features, out_grad)], axis=0
    )
    own = lax.ppermute(quarter, PLANE, swap_pairs())
    near, far = pl.BlockSpec(memory_space=pltpu.VMEM), pl.BlockSpec(memory_space=pl.ANY)
    plane = pl.pallas_call(
        words_body,
        out_shape=jax.ShapeDtypeStruct((K8, 160, W), BF),
        in_specs=[near, far, far],
        out_specs=near,
        scratch_shapes=[
            pltpu.VMEM((512, 128), I32),
            pltpu.VMEM((128, W), BF),
            pltpu.SemaphoreType.DMA((2,)),
        ],
        compiler_params=PARAMS,
    )(back_place.reshape(1, 32), back_bits.reshape(512, 128), features)
    plane = lax.all_to_all(plane, ROWS2, 0, 0)
    parts = call(forward_body, jax.ShapeDtypeStruct((Z, 40, W), BF), plane)
    parts = lax.all_to_all(parts, "z", 0, 0)
    act, hidden_grad, pushed, term = call(
        middle_body,
        (
            jax.ShapeDtypeStruct((Q, W), BF),
            jax.ShapeDtypeStruct((Q, W), F32),
            jax.ShapeDtypeStruct((Q, W), BF),
            jax.ShapeDtypeStruct((W, W), BF),
        ),
        parts,
        own,
        weight,
    )
    act = lax.ppermute(act, PLANE, swap_pairs())
    terms = lax.all_to_all(term.reshape(PL, 8, W), PLANE, 0, 0)
    sent = call(send_body, jax.ShapeDtypeStruct((Z, 40, W), BF), terms, pushed)
    gathered = lax.all_to_all(sent, "z", 0, 0)
    parts = pl.pallas_call(
        backward_body,
        out_shape=jax.ShapeDtypeStruct((K8, 144, W), BF),
        in_specs=[near] * 3,
        out_specs=near,
        scratch_shapes=[pltpu.VMEM((K8, 128, W), F32)],
        compiler_params=PARAMS,
    )(plane, gathered, hidden_grad)
    parts = lax.all_to_all(parts, ROWS2, 0, 0)
    share = call(share_body, jax.ShapeDtypeStruct((288, W), BF), parts, act)
    shares = lax.all_gather(share, REP, axis=0)
    return call(
        finish_body,
        (
            jax.ShapeDtypeStruct((4 * Q, W), BF),
            jax.ShapeDtypeStruct((W, W), F32),
            jax.ShapeDtypeStruct((4 * Q, W), BF),
        ),
        shares,
    )


def solution(mesh):
    fine = Mesh(mesh.devices.reshape(16, 4, 2, 2, 2), ("z", "x", "yl", "yh", "c"))
    return jax.shard_map(
        per_device,
        mesh=fine,
        in_specs=(
            P(NODE, None),
            P(),
            P(NODE, None),
            P(NODE, REP, None),
            P(NODE, REP, None, None, None),
            P(NODE, REP, None),
            P(NODE, REP, None, None, None),
        ),
        out_specs=(P(NODE, None), P(), P(NODE, None)),
        check_vma=False,
    )
```

```python
import jax
import jax.numpy as jnp
from jax import lax
from jax.experimental import pallas as pl
from jax.experimental.pallas import tpu as pltpu
from jax.sharding import Mesh, PartitionSpec as P

BF, F32, I32 = jnp.bfloat16, jnp.float32, jnp.int32
NODE, REP = ("z", "x", "yl"), ("yh", "c")
ROWS2, PLANE = ("x", "yl"), ("x", "yl", "yh", "c")
Z, K8, R4, PL = 16, 8, 4, 32
Q, W = 32, 256
PARAMS = pltpu.CompilerParams(vmem_limit_bytes=24 * 1024 * 1024)


FULL = 62 * 1024 * 1024


def where_am_i():
    x = lax.axis_index("x")
    q = (x % 2) * 2 + lax.axis_index("yl")
    return x // 2, q, lax.axis_index("yh") * 2 + lax.axis_index("c")


def swap_pairs():
    pairs = []
    for x1 in range(2):
        for a in range(4):
            for b in range(4):
                pairs.append((x1 * 16 + a * 4 + b, x1 * 16 + b * 4 + a))
    return pairs


def call(body, shapes, *args):
    return pl.pallas_call(
        body,
        out_shape=shapes,
        in_specs=[pl.BlockSpec(memory_space=pltpu.VMEM)] * len(args),
        out_specs=jax.tree.map(lambda _: pl.BlockSpec(memory_space=pltpu.VMEM), shapes),
        compiler_params=PARAMS,
    )(*args)


def words_body(place_far, bits_far, features_far, grads_far, out, place, bits, features, grads, sems):
    fetches = [
        pltpu.make_async_copy(place_far, place, sems.at[0]),
        pltpu.make_async_copy(bits_far, bits, sems.at[1]),
        pltpu.make_async_copy(features_far, features, sems.at[2]),
        pltpu.make_async_copy(grads_far, grads, sems.at[3]),
    ]
    for fetch in fetches:
        fetch.start()
    row = lax.broadcasted_iota(I32, (512, 512), 0)
    want = (((row // 4) % 16) * 2 + row // 256) * 16 + ((row // 64) % 4) * 4 + row % 4
    lane = lax.broadcasted_iota(I32, (32, 512), 1)
    spread = jnp.where(lane // 16 == lax.broadcasted_iota(I32, (32, 512), 0), 1.0, 0.0).astype(BF)
    column = lax.broadcasted_iota(I32, (8, 512), 1) % 16
    fetches[0].wait()
    at = jnp.broadcast_to(place[...].astype(F32), (8, 32)).astype(BF)
    key = jnp.dot(at, spread, preferred_element_type=F32).astype(I32) * 16 + column
    hot = jnp.where(want == key[0:1, :], 1.0, 0.0).astype(BF)
    fetches[1].wait()
    dense = jnp.dot(hot, bits[...].astype(F32).astype(BF), preferred_element_type=F32).astype(BF)
    for k in range(K8):
        out[k, 0:32, 0:128] = dense[k * 64 : k * 64 + 32]
        out[k, 0:32, 128:256] = dense[k * 64 + 32 : k * 64 + 64]
    fetches[2].wait()
    fetches[3].wait()
    for k in range(K8):
        out[k, 32:160, :] = features[...]
        out[k, 160:192, :] = grads[(k % 4) * 32 : (k % 4) * 32 + 32, :]


def unpacked(words):
    halves = []
    for h in range(2):
        half = words[:, h * 128 : (h + 1) * 128].astype(F32).astype(I32)
        spread = jnp.broadcast_to(half[:, None, :], (32, 8, 128))
        bits = jnp.bitwise_and(jnp.right_shift(spread, lax.broadcasted_iota(I32, (32, 8, 128), 1)), 1)
        halves.append(bits.reshape(256, 128).astype(F32).astype(BF))
    return jnp.concatenate(halves, axis=0)


def over_rows(block, source):
    return lax.dot_general(block, source, (((0,), (0,)), ((), ())), preferred_element_type=F32)


def forward_body(plane, out, own):
    block = jnp.concatenate([unpacked(plane[k, 0:32, :]) for k in range(K8)], axis=1)
    source = plane[:, 32:160, :].reshape(K8 * 128, W)
    part = jnp.dot(block, source, preferred_element_type=F32)
    fourth = lax.broadcasted_iota(I32, (16, 1024), 1) // 256
    ones = jnp.where(fourth == lax.broadcasted_iota(I32, (16, 1024), 0), 1.0, 0.0).astype(BF)
    degree = lax.dot_general(ones, block, (((1,), (1,)), ((), ())), preferred_element_type=F32)
    for z in range(Z):
        lanes = degree[0:8, (z // 4) * 128 : (z // 4 + 1) * 128]
        tail = jnp.concatenate([lanes, jnp.zeros_like(lanes)], axis=1)
        out[z] = jnp.concatenate([part[z * 32 : (z + 1) * 32], tail], axis=0).astype(BF)
    x1, q, r = where_am_i()
    own[0:32, :] = plane[x1 * 4 + r, pl.ds(pl.multiple_of(32 + q * 32, 32), 32), :]
    own[32:64, :] = plane[x1 * 4 + r, 160:192, :]


def middle_body(parts, own, weight, act, back, pushed, term):
    total = jnp.sum(parts[...].astype(F32), axis=0)
    degree = jnp.sum(total[32:36, 0:128], axis=0, keepdims=True)
    first = (lax.axis_index("z") % 4) * 32
    pick = lax.broadcasted_iota(I32, (32, 128), 1) == lax.broadcasted_iota(I32, (32, 128), 0) + first
    counted = jnp.sum(jnp.where(pick, degree, 0.0), axis=1, keepdims=True)
    scaling = lax.rsqrt(1.0 + counted)
    hidden = (own[0:32, :].astype(F32) + total[0:32] * scaling).astype(BF)
    logits = jnp.dot(hidden, weight[...], preferred_element_type=F32)
    gate = jax.nn.sigmoid(logits)
    act[...] = (logits * gate).astype(BF)
    upstream = (own[32:64, :].astype(F32) * gate * (1.0 + logits * (1.0 - gate))).astype(BF)
    hidden_grad = lax.dot_general(
        upstream, weight[...], (((1,), (1,)), ((), ())), preferred_element_type=F32
    )
    back[...] = hidden_grad
    pushed[...] = (hidden_grad * scaling).astype(BF)
    term[...] = over_rows(hidden, upstream).astype(BF)


def send_body(terms, pushed, out):
    extra = jnp.sum(terms[...].astype(F32), axis=0)
    message = jnp.concatenate([pushed[...].astype(F32), extra], axis=0).astype(BF)
    for z in range(Z):
        out[z] = message


def backward_body(plane, gathered, hidden_grad, out, total):
    x1, q, r = where_am_i()
    received = gathered[...].astype(F32)
    source = received[:, 0:32].reshape(Z * Q, W).astype(BF)
    extra = jnp.sum(received[:, 32:40], axis=0)
    for k in range(K8):
        total[k] = over_rows(unpacked(plane[k, 0:32, :]), source)
    rows = pl.ds(pl.multiple_of(q * 32, 32), 32)
    total[x1 * 4 + r, rows, :] = total[x1 * 4 + r, rows, :] + hidden_grad[...]
    for k in range(K8):
        out[k] = jnp.concatenate([total[k], extra], axis=0).astype(BF)


def share_body(parts, act, out):
    values = parts[...].astype(F32)
    out[0:128, :] = jnp.sum(values[:, 0:128], axis=0).astype(BF)
    out[128:192, :] = values[:, 128:136].reshape(64, W).astype(BF)
    out[192:224, :] = act[...]


def finish_body(shares, activation, weight_grad, input_grad):
    input_grad[...] = jnp.sum(shares[:, 0:128, :].astype(F32), axis=0).astype(BF)
    for r in range(R4):
        activation[r * 32 : (r + 1) * 32, :] = shares[r, 192:224, :]
        slices = shares[r, 128:192, :].astype(F32)
        for k in range(K8):
            weight_grad[k * 32 + r * 8 : k * 32 + r * 8 + 8, :] = slices[k * 8 : k * 8 + 8]


def per_device(features, weight, out_grad, tile_place, tile_bits, back_place, back_bits):
    near, far = pl.BlockSpec(memory_space=pltpu.VMEM), pl.BlockSpec(memory_space=pltpu.HBM)
    plane = pl.pallas_call(
        words_body,
        out_shape=jax.ShapeDtypeStruct((K8, 192, W), BF),
        in_specs=[far] * 4,
        out_specs=near,
        scratch_shapes=[
            pltpu.VMEM((1, 32), I32),
            pltpu.VMEM((512, 128), I32),
            pltpu.VMEM((128, W), BF),
            pltpu.VMEM((128, W), BF),
            pltpu.SemaphoreType.DMA((4,)),
        ],
        compiler_params=pltpu.CompilerParams(vmem_limit_bytes=FULL),
    )(back_place.reshape(1, 32), back_bits.reshape(512, 128), features, out_grad)
    plane = lax.all_to_all(plane, ROWS2, 0, 0)
    parts, own = call(
        forward_body,
        (jax.ShapeDtypeStruct((Z, 40, W), BF), jax.ShapeDtypeStruct((2 * Q, W), BF)),
        plane,
    )
    parts = lax.all_to_all(parts, "z", 0, 0)
    act, hidden_grad, pushed, term = call(
        middle_body,
        (
            jax.ShapeDtypeStruct((Q, W), BF),
            jax.ShapeDtypeStruct((Q, W), F32),
            jax.ShapeDtypeStruct((Q, W), BF),
            jax.ShapeDtypeStruct((W, W), BF),
        ),
        parts,
        own,
        weight,
    )
    act = lax.ppermute(act, PLANE, swap_pairs())
    terms = lax.all_to_all(term.reshape(PL, 8, W), PLANE, 0, 0)
    sent = call(send_body, jax.ShapeDtypeStruct((Z, 40, W), BF), terms, pushed)
    gathered = lax.all_to_all(sent, "z", 0, 0)
    parts = pl.pallas_call(
        backward_body,
        out_shape=jax.ShapeDtypeStruct((K8, 136, W), BF),
        in_specs=[near] * 3,
        out_specs=near,
        scratch_shapes=[pltpu.VMEM((K8, 128, W), F32)],
        compiler_params=PARAMS,
    )(plane, gathered, hidden_grad)
    parts = lax.all_to_all(parts, ROWS2, 0, 0)
    share = call(share_body, jax.ShapeDtypeStruct((224, W), BF), parts, act)
    shares = lax.all_gather(share, REP, axis=0)
    return call(
        finish_body,
        (
            jax.ShapeDtypeStruct((4 * Q, W), BF),
            jax.ShapeDtypeStruct((W, W), F32),
            jax.ShapeDtypeStruct((4 * Q, W), BF),
        ),
        shares,
    )


def solution(mesh):
    fine = Mesh(mesh.devices.reshape(16, 4, 2, 2, 2), ("z", "x", "yl", "yh", "c"))
    return jax.shard_map(
        per_device,
        mesh=fine,
        in_specs=(
            P(NODE, None),
            P(),
            P(NODE, None),
            P(NODE, REP, None),
            P(NODE, REP, None, None, None),
            P(NODE, REP, None),
            P(NODE, REP, None, None, None),
        ),
        out_specs=(P(NODE, None), P(), P(NODE, None)),
        check_vma=False,
    )
```

```python
import jax
import jax.numpy as jnp
from jax import lax
from jax.experimental import pallas as pl
from jax.experimental.pallas import tpu as pltpu
from jax.sharding import Mesh, PartitionSpec as P

BF, F32, I32 = jnp.bfloat16, jnp.float32, jnp.int32
NODE, REP = ("z", "x", "yl"), ("yh", "c")
ROWS2, PLANE = ("x", "yl"), ("x", "yl", "yh", "c")
Z, K8, R4, PL = 16, 8, 4, 32
Q, W = 32, 256
PARAMS = pltpu.CompilerParams(vmem_limit_bytes=24 * 1024 * 1024)


FULL = 62 * 1024 * 1024


def where_am_i():
    x = lax.axis_index("x")
    q = (x % 2) * 2 + lax.axis_index("yl")
    return x // 2, q, lax.axis_index("yh") * 2 + lax.axis_index("c")


def swap_pairs():
    pairs = []
    for x1 in range(2):
        for a in range(4):
            for b in range(4):
                pairs.append((x1 * 16 + a * 4 + b, x1 * 16 + b * 4 + a))
    return pairs


def call(body, shapes, *args):
    return pl.pallas_call(
        body,
        out_shape=shapes,
        in_specs=[pl.BlockSpec(memory_space=pltpu.VMEM)] * len(args),
        out_specs=jax.tree.map(lambda _: pl.BlockSpec(memory_space=pltpu.VMEM), shapes),
        compiler_params=PARAMS,
    )(*args)


def words_body(place_far, bits_far, features_far, grads_far, out, place, bits, features, grads, sems):
    fetches = [
        pltpu.make_async_copy(place_far, place, sems.at[0]),
        pltpu.make_async_copy(features_far, features, sems.at[1]),
        pltpu.make_async_copy(grads_far, grads, sems.at[2]),
        pltpu.make_async_copy(bits_far, bits, sems.at[3]),
    ]
    for fetch in fetches:
        fetch.start()
    row = lax.broadcasted_iota(I32, (512, 128), 0)
    want = (((row // 4) % 16) * 2 + row // 256) * 16 + ((row // 64) % 4) * 4 + row % 4
    lane = lax.broadcasted_iota(I32, (32, 512), 1)
    spread = jnp.where(lane // 16 == lax.broadcasted_iota(I32, (32, 512), 0), 1.0, 0.0).astype(BF)
    column = lax.broadcasted_iota(I32, (8, 512), 1) % 16
    fetches[0].wait()
    at = jnp.broadcast_to(place[...].astype(F32), (8, 32)).astype(BF)
    key = jnp.dot(at, spread, preferred_element_type=F32).astype(I32) * 16 + column
    hot = jnp.concatenate(
        [jnp.where(want == key[0:1, c * 128 : (c + 1) * 128], 1.0, 0.0) for c in range(4)], axis=1
    ).astype(BF)
    fetches[1].wait()
    fetches[2].wait()
    for k in range(K8):
        out[k, 32:160, :] = features[...]
        out[k, 160:192, :] = grads[(k % 4) * 32 : (k % 4) * 32 + 32, :]
    fetches[3].wait()
    dense = jnp.dot(hot, bits[...].astype(F32).astype(BF), preferred_element_type=F32).astype(BF)
    for k in range(K8):
        out[k, 0:32, 0:128] = dense[k * 64 : k * 64 + 32]
        out[k, 0:32, 128:256] = dense[k * 64 + 32 : k * 64 + 64]


def unpacked(words):
    halves = []
    for h in range(2):
        half = words[:, h * 128 : (h + 1) * 128].astype(F32).astype(I32)
        spread = jnp.broadcast_to(half[:, None, :], (32, 8, 128))
        bits = jnp.bitwise_and(jnp.right_shift(spread, lax.broadcasted_iota(I32, (32, 8, 128), 1)), 1)
        halves.append(bits.reshape(256, 128).astype(F32).astype(BF))
    return jnp.concatenate(halves, axis=0)


def over_rows(block, source):
    return lax.dot_general(block, source, (((0,), (0,)), ((), ())), preferred_element_type=F32)


def forward_body(plane, out, own):
    block = jnp.concatenate([unpacked(plane[k, 0:32, :]) for k in range(K8)], axis=1)
    source = plane[:, 32:160, :].reshape(K8 * 128, W)
    part = jnp.dot(block, source, preferred_element_type=F32)
    fourth = lax.broadcasted_iota(I32, (16, 1024), 1) // 256
    ones = jnp.where(fourth == lax.broadcasted_iota(I32, (16, 1024), 0), 1.0, 0.0).astype(BF)
    degree = lax.dot_general(ones, block, (((1,), (1,)), ((), ())), preferred_element_type=F32)
    for z in range(Z):
        mine = part[z * 32 : (z + 1) * 32]
        lanes = degree[0:8, (z // 4) * 128 : (z // 4 + 1) * 128]
        out[z] = jnp.concatenate([mine[:, 0:128], mine[:, 128:256], lanes], axis=0).astype(BF)
    x1, q, r = where_am_i()
    own[0:32, :] = plane[x1 * 4 + r, pl.ds(pl.multiple_of(32 + q * 32, 32), 32), :]
    own[32:64, :] = plane[x1 * 4 + r, 160:192, :]


def middle_body(parts, own, weight, act, back, pushed, term):
    total = jnp.sum(parts[...].astype(F32), axis=0)
    degree = jnp.sum(total[64:68], axis=0, keepdims=True)
    first = (lax.axis_index("z") % 4) * 32
    pick = lax.broadcasted_iota(I32, (32, 128), 1) == lax.broadcasted_iota(I32, (32, 128), 0) + first
    counted = jnp.sum(jnp.where(pick, degree, 0.0), axis=1, keepdims=True)
    scaling = lax.rsqrt(1.0 + counted)
    gathered = jnp.concatenate([total[0:32], total[32:64]], axis=1)
    hidden = (own[0:32, :].astype(F32) + gathered * scaling).astype(BF)
    logits = jnp.dot(hidden, weight[...], preferred_element_type=F32)
    gate = jax.nn.sigmoid(logits)
    act[...] = (logits * gate).astype(BF)
    upstream = (own[32:64, :].astype(F32) * gate * (1.0 + logits * (1.0 - gate))).astype(BF)
    hidden_grad = lax.dot_general(
        upstream, weight[...], (((1,), (1,)), ((), ())), preferred_element_type=F32
    )
    back[...] = hidden_grad
    pushed[...] = (hidden_grad * scaling).astype(BF)
    term[...] = over_rows(hidden, upstream).astype(BF)


def send_body(terms, pushed, out):
    extra = jnp.sum(terms[...].astype(F32), axis=0)
    message = jnp.concatenate([pushed[...].astype(F32), extra], axis=0).astype(BF)
    for z in range(Z):
        out[z] = message


def backward_body(plane, gathered, hidden_grad, out):
    x1, q, r = where_am_i()
    received = gathered[...]
    source = received[:, 0:32].reshape(Z * Q, W)
    extra = jnp.sum(received[:, 32:40].astype(F32), axis=0)
    own = hidden_grad[...]
    placed = jnp.concatenate([jnp.where(q == t, own, 0.0) for t in range(4)], axis=0)
    for k in range(K8):
        part = over_rows(unpacked(plane[k, 0:32, :]), source)
        part = part + jnp.where(x1 * 4 + r == k, placed, 0.0)
        out[k] = jnp.concatenate([part, extra], axis=0).astype(BF)


def share_body(parts, act, out):
    values = parts[...].astype(F32)
    out[0:128, :] = jnp.sum(values[:, 0:128], axis=0).astype(BF)
    out[128:192, :] = values[:, 128:136].reshape(64, W).astype(BF)
    out[192:224, :] = act[...]


def finish_body(shares, activation, weight_grad, input_grad):
    input_grad[...] = jnp.sum(shares[:, 0:128, :].astype(F32), axis=0).astype(BF)
    for r in range(R4):
        activation[r * 32 : (r + 1) * 32, :] = shares[r, 192:224, :]
        slices = shares[r, 128:192, :].astype(F32)
        for k in range(K8):
            weight_grad[k * 32 + r * 8 : k * 32 + r * 8 + 8, :] = slices[k * 8 : k * 8 + 8]


def per_device(features, weight, out_grad, tile_place, tile_bits, back_place, back_bits):
    near, far = pl.BlockSpec(memory_space=pltpu.VMEM), pl.BlockSpec(memory_space=pltpu.HBM)
    plane = pl.pallas_call(
        words_body,
        out_shape=jax.ShapeDtypeStruct((K8, 192, W), BF),
        in_specs=[far] * 4,
        out_specs=near,
        scratch_shapes=[
            pltpu.VMEM((1, 32), I32),
            pltpu.VMEM((512, 128), I32),
            pltpu.VMEM((128, W), BF),
            pltpu.VMEM((128, W), BF),
            pltpu.SemaphoreType.DMA((4,)),
        ],
        compiler_params=pltpu.CompilerParams(vmem_limit_bytes=FULL),
    )(back_place.reshape(1, 32), back_bits.reshape(512, 128), features, out_grad)
    plane = lax.all_to_all(plane, ROWS2, 0, 0)
    parts, own = call(
        forward_body,
        (jax.ShapeDtypeStruct((Z, 72, 128), BF), jax.ShapeDtypeStruct((2 * Q, W), BF)),
        plane,
    )
    parts = lax.all_to_all(parts, "z", 0, 0)
    act, hidden_grad, pushed, term = call(
        middle_body,
        (
            jax.ShapeDtypeStruct((Q, W), BF),
            jax.ShapeDtypeStruct((Q, W), F32),
            jax.ShapeDtypeStruct((Q, W), BF),
            jax.ShapeDtypeStruct((W, W), BF),
        ),
        parts,
        own,
        weight,
    )
    act = lax.ppermute(act, PLANE, swap_pairs())
    terms = lax.all_to_all(term.reshape(PL, 8, W), PLANE, 0, 0)
    sent = call(send_body, jax.ShapeDtypeStruct((Z, 40, W), BF), terms, pushed)
    gathered = lax.all_to_all(sent, "z", 0, 0)
    parts = call(
        backward_body, jax.ShapeDtypeStruct((K8, 136, W), BF), plane, gathered, hidden_grad
    )
    parts = lax.all_to_all(parts, ROWS2, 0, 0)
    share = call(share_body, jax.ShapeDtypeStruct((224, W), BF), parts, act)
    shares = lax.all_gather(share, REP, axis=0)
    return call(
        finish_body,
        (
            jax.ShapeDtypeStruct((4 * Q, W), BF),
            jax.ShapeDtypeStruct((W, W), F32),
            jax.ShapeDtypeStruct((4 * Q, W), BF),
        ),
        shares,
    )


def solution(mesh):
    fine = Mesh(mesh.devices.reshape(16, 4, 2, 2, 2), ("z", "x", "yl", "yh", "c"))
    return jax.shard_map(
        per_device,
        mesh=fine,
        in_specs=(
            P(NODE, None),
            P(),
            P(NODE, None),
            P(NODE, REP, None),
            P(NODE, REP, None, None, None),
            P(NODE, REP, None),
            P(NODE, REP, None, None, None),
        ),
        out_specs=(P(NODE, None), P(), P(NODE, None)),
        check_vma=False,
    )
```

```python
import jax
import jax.numpy as jnp
from jax import lax
from jax.experimental import pallas as pl
from jax.experimental.pallas import tpu as pltpu
from jax.sharding import Mesh, PartitionSpec as P

BF, F32, I32 = jnp.bfloat16, jnp.float32, jnp.int32
NODE, REP = ("z", "x", "yl"), ("yh", "c")
ROWS2, PLANE = ("x", "yl"), ("x", "yl", "yh", "c")
Z, K8, R4, PL = 16, 8, 4, 32
Q, W = 32, 256
PARAMS = pltpu.CompilerParams(vmem_limit_bytes=24 * 1024 * 1024)


FULL = 62 * 1024 * 1024


def where_am_i():
    x = lax.axis_index("x")
    q = (x % 2) * 2 + lax.axis_index("yl")
    return x // 2, q, lax.axis_index("yh") * 2 + lax.axis_index("c")


def swap_pairs():
    pairs = []
    for x1 in range(2):
        for a in range(4):
            for b in range(4):
                pairs.append((x1 * 16 + a * 4 + b, x1 * 16 + b * 4 + a))
    return pairs


def call(body, shapes, *args):
    return pl.pallas_call(
        body,
        out_shape=shapes,
        in_specs=[pl.BlockSpec(memory_space=pltpu.VMEM)] * len(args),
        out_specs=jax.tree.map(lambda _: pl.BlockSpec(memory_space=pltpu.VMEM), shapes),
        compiler_params=PARAMS,
    )(*args)


def words_body(place_far, bits_far, features_far, grads_far, out, place, bits, features, grads, words, sems):
    fetches = [
        pltpu.make_async_copy(place_far, place, sems.at[0]),
        pltpu.make_async_copy(features_far, features, sems.at[1]),
        pltpu.make_async_copy(grads_far, grads, sems.at[2]),
        pltpu.make_async_copy(bits_far, bits, sems.at[3]),
    ]
    for fetch in fetches:
        fetch.start()
    row = lax.broadcasted_iota(I32, (512, 128), 0)
    want = (((row // 4) % 16) * 2 + row // 256) * 16 + ((row // 64) % 4) * 4 + row % 4
    lane = lax.broadcasted_iota(I32, (32, 512), 1)
    spread = jnp.where(lane // 16 == lax.broadcasted_iota(I32, (32, 512), 0), 1.0, 0.0).astype(BF)
    column = lax.broadcasted_iota(I32, (8, 512), 1) % 16
    fetches[0].wait()
    at = jnp.broadcast_to(place[...].astype(F32), (8, 32)).astype(BF)
    key = jnp.dot(at, spread, preferred_element_type=F32).astype(I32) * 16 + column
    hot = jnp.concatenate(
        [jnp.where(want == key[0:1, c * 128 : (c + 1) * 128], 1.0, 0.0) for c in range(4)], axis=1
    ).astype(BF)
    fetches[1].wait()
    fetches[2].wait()
    puts = []
    for k in range(K8):
        quarter = grads.at[pl.ds((k % 4) * 32, 32), :]
        puts.append(pltpu.make_async_copy(features, out.at[k, pl.ds(32, 128), :], sems.at[4 + k]))
        puts.append(pltpu.make_async_copy(quarter, out.at[k, pl.ds(160, 32), :], sems.at[12 + k]))
    for put in puts:
        put.start()
    fetches[3].wait()
    dense = jnp.dot(hot, bits[...].astype(F32).astype(BF), preferred_element_type=F32).astype(BF)
    for k in range(K8):
        words[k, :, 0:128] = dense[k * 64 : k * 64 + 32]
        words[k, :, 128:256] = dense[k * 64 + 32 : k * 64 + 64]
    last = pltpu.make_async_copy(words, out.at[:, pl.ds(0, 32), :], sems.at[20])
    last.start()
    for put in puts:
        put.wait()
    last.wait()


def unpacked(words):
    halves = []
    for h in range(2):
        half = words[:, h * 128 : (h + 1) * 128].astype(F32).astype(I32)
        spread = jnp.broadcast_to(half[:, None, :], (32, 8, 128))
        bits = jnp.bitwise_and(jnp.right_shift(spread, lax.broadcasted_iota(I32, (32, 8, 128), 1)), 1)
        halves.append(bits.reshape(256, 128).astype(F32).astype(BF))
    return jnp.concatenate(halves, axis=0)


def over_rows(block, source):
    return lax.dot_general(block, source, (((0,), (0,)), ((), ())), preferred_element_type=F32)


def forward_body(plane, out, own, turned):
    block = jnp.concatenate([unpacked(plane[k, 0:32, :]) for k in range(K8)], axis=1)
    source = plane[:, 32:160, :].reshape(K8 * 128, W)
    part = jnp.dot(block, source, preferred_element_type=F32)
    fourth = lax.broadcasted_iota(I32, (16, 1024), 1) // 256
    ones = jnp.where(fourth == lax.broadcasted_iota(I32, (16, 1024), 0), 1.0, 0.0).astype(BF)
    degree = lax.dot_general(ones, block, (((1,), (1,)), ((), ())), preferred_element_type=F32)
    for z in range(Z):
        mine = part[z * 32 : (z + 1) * 32]
        lanes = degree[0:8, (z // 4) * 128 : (z // 4 + 1) * 128]
        out[z] = jnp.concatenate([mine[:, 0:128], mine[:, 128:256], lanes], axis=0).astype(BF)
    x1, q, r = where_am_i()
    own[0:32, :] = plane[x1 * 4 + r, pl.ds(pl.multiple_of(32 + q * 32, 32), 32), :]
    own[32:64, :] = plane[x1 * 4 + r, 160:192, :]
    turned[...] = block.T


def middle_body(parts, own, weight, act, back, pushed, term):
    total = jnp.sum(parts[...].astype(F32), axis=0)
    degree = jnp.sum(total[64:68], axis=0, keepdims=True)
    first = (lax.axis_index("z") % 4) * 32
    pick = lax.broadcasted_iota(I32, (32, 128), 1) == lax.broadcasted_iota(I32, (32, 128), 0) + first
    counted = jnp.sum(jnp.where(pick, degree, 0.0), axis=1, keepdims=True)
    scaling = lax.rsqrt(1.0 + counted)
    gathered = jnp.concatenate([total[0:32], total[32:64]], axis=1)
    hidden = (own[0:32, :].astype(F32) + gathered * scaling).astype(BF)
    logits = jnp.dot(hidden, weight[...], preferred_element_type=F32)
    gate = jax.nn.sigmoid(logits)
    act[...] = (logits * gate).astype(BF)
    upstream = (own[32:64, :].astype(F32) * gate * (1.0 + logits * (1.0 - gate))).astype(BF)
    hidden_grad = lax.dot_general(
        upstream, weight[...], (((1,), (1,)), ((), ())), preferred_element_type=F32
    )
    back[...] = hidden_grad
    pushed[...] = (hidden_grad * scaling).astype(BF)
    term[...] = over_rows(hidden, upstream).astype(BF)


def send_body(terms, pushed, out):
    extra = jnp.sum(terms[...].astype(F32), axis=0)
    message = jnp.concatenate([pushed[...].astype(F32), extra], axis=0).astype(BF)
    for z in range(Z):
        out[z] = message


def backward_body(turned, gathered, hidden_grad, out):
    x1, q, r = where_am_i()
    received = gathered[...]
    source = received[:, 0:32].reshape(Z * Q, W)
    extra = jnp.sum(received[:, 32:40].astype(F32), axis=0)
    own = hidden_grad[...]
    placed = jnp.concatenate([jnp.where(q == t, own, 0.0) for t in range(4)], axis=0)
    for k in range(K8):
        part = jnp.dot(turned[k * 128 : (k + 1) * 128, :], source, preferred_element_type=F32)
        part = part + jnp.where(x1 * 4 + r == k, placed, 0.0)
        out[k] = jnp.concatenate([part, extra], axis=0).astype(BF)


def share_body(parts, act, out):
    values = parts[...].astype(F32)
    out[0:128, :] = jnp.sum(values[:, 0:128], axis=0).astype(BF)
    out[128:192, :] = values[:, 128:136].reshape(64, W).astype(BF)
    out[192:224, :] = act[...]


def finish_body(shares, activation, weight_grad, input_grad):
    input_grad[...] = jnp.sum(shares[:, 0:128, :].astype(F32), axis=0).astype(BF)
    for r in range(R4):
        activation[r * 32 : (r + 1) * 32, :] = shares[r, 192:224, :]
        slices = shares[r, 128:192, :].astype(F32)
        for k in range(K8):
            weight_grad[k * 32 + r * 8 : k * 32 + r * 8 + 8, :] = slices[k * 8 : k * 8 + 8]


def per_device(features, weight, out_grad, tile_place, tile_bits, back_place, back_bits):
    near, far = pl.BlockSpec(memory_space=pltpu.VMEM), pl.BlockSpec(memory_space=pltpu.HBM)
    plane = pl.pallas_call(
        words_body,
        out_shape=jax.ShapeDtypeStruct((K8, 192, W), BF),
        in_specs=[far] * 4,
        out_specs=far,
        scratch_shapes=[
            pltpu.VMEM((1, 32), I32),
            pltpu.VMEM((512, 128), I32),
            pltpu.VMEM((128, W), BF),
            pltpu.VMEM((128, W), BF),
            pltpu.VMEM((K8, 32, W), BF),
            pltpu.SemaphoreType.DMA((21,)),
        ],
        compiler_params=pltpu.CompilerParams(vmem_limit_bytes=FULL),
    )(back_place.reshape(1, 32), back_bits.reshape(512, 128), features, out_grad)
    plane = lax.all_to_all(plane, ROWS2, 0, 0)
    parts, own, turned = call(
        forward_body,
        (
            jax.ShapeDtypeStruct((Z, 72, 128), BF),
            jax.ShapeDtypeStruct((2 * Q, W), BF),
            jax.ShapeDtypeStruct((K8 * 128, Z * Q), BF),
        ),
        plane,
    )
    parts = lax.all_to_all(parts, "z", 0, 0)
    act, hidden_grad, pushed, term = call(
        middle_body,
        (
            jax.ShapeDtypeStruct((Q, W), BF),
            jax.ShapeDtypeStruct((Q, W), F32),
            jax.ShapeDtypeStruct((Q, W), BF),
            jax.ShapeDtypeStruct((W, W), BF),
        ),
        parts,
        own,
        weight,
    )
    act = lax.ppermute(act, PLANE, swap_pairs())
    terms = lax.all_to_all(term.reshape(PL, 8, W), PLANE, 0, 0)
    sent = call(send_body, jax.ShapeDtypeStruct((Z, 40, W), BF), terms, pushed)
    gathered = lax.all_to_all(sent, "z", 0, 0)
    parts = call(
        backward_body, jax.ShapeDtypeStruct((K8, 136, W), BF), turned, gathered, hidden_grad
    )
    parts = lax.all_to_all(parts, ROWS2, 0, 0)
    share = call(share_body, jax.ShapeDtypeStruct((224, W), BF), parts, act)
    shares = lax.all_gather(share, REP, axis=0)
    return call(
        finish_body,
        (
            jax.ShapeDtypeStruct((4 * Q, W), BF),
            jax.ShapeDtypeStruct((W, W), F32),
            jax.ShapeDtypeStruct((4 * Q, W), BF),
        ),
        shares,
    )


def solution(mesh):
    fine = Mesh(mesh.devices.reshape(16, 4, 2, 2, 2), ("z", "x", "yl", "yh", "c"))
    return jax.shard_map(
        per_device,
        mesh=fine,
        in_specs=(
            P(NODE, None),
            P(),
            P(NODE, None),
            P(NODE, REP, None),
            P(NODE, REP, None, None, None),
            P(NODE, REP, None),
            P(NODE, REP, None, None, None),
        ),
        out_specs=(P(NODE, None), P(), P(NODE, None)),
        check_vma=False,
    )
```

```python
import jax
import jax.numpy as jnp
from jax import lax
from jax.experimental import pallas as pl
from jax.experimental.pallas import tpu as pltpu
from jax.sharding import Mesh, PartitionSpec as P

BF, F32, I32 = jnp.bfloat16, jnp.float32, jnp.int32
NODE, REP = ("z", "x", "yl"), ("yh", "c")
ROWS2, PLANE = ("x", "yl"), ("x", "yl", "yh", "c")
Z, K8, R4, PL = 16, 8, 4, 32
Q, W = 32, 256
PARAMS = pltpu.CompilerParams(vmem_limit_bytes=24 * 1024 * 1024)


FULL = 62 * 1024 * 1024


def where_am_i():
    x = lax.axis_index("x")
    q = (x % 2) * 2 + lax.axis_index("yl")
    return x // 2, q, lax.axis_index("yh") * 2 + lax.axis_index("c")


def swap_pairs():
    pairs = []
    for x1 in range(2):
        for a in range(4):
            for b in range(4):
                pairs.append((x1 * 16 + a * 4 + b, x1 * 16 + b * 4 + a))
    return pairs


def call(body, shapes, *args):
    return pl.pallas_call(
        body,
        out_shape=shapes,
        in_specs=[pl.BlockSpec(memory_space=pltpu.VMEM)] * len(args),
        out_specs=jax.tree.map(lambda _: pl.BlockSpec(memory_space=pltpu.VMEM), shapes),
        compiler_params=PARAMS,
    )(*args)


def words_body(place_far, bits_far, features_far, out, place, bits, features, words, sems):
    fetches = [
        pltpu.make_async_copy(place_far, place, sems.at[0]),
        pltpu.make_async_copy(features_far, features, sems.at[1]),
        pltpu.make_async_copy(bits_far, bits, sems.at[3]),
    ]
    for fetch in fetches:
        fetch.start()
    row = lax.broadcasted_iota(I32, (512, 128), 0)
    want = (((row // 4) % 16) * 2 + row // 256) * 16 + ((row // 64) % 4) * 4 + row % 4
    lane = lax.broadcasted_iota(I32, (32, 512), 1)
    spread = jnp.where(lane // 16 == lax.broadcasted_iota(I32, (32, 512), 0), 1.0, 0.0).astype(BF)
    column = lax.broadcasted_iota(I32, (8, 512), 1) % 16
    fetches[0].wait()
    at = jnp.broadcast_to(place[...].astype(F32), (8, 32)).astype(BF)
    key = jnp.dot(at, spread, preferred_element_type=F32).astype(I32) * 16 + column
    hot = jnp.concatenate(
        [jnp.where(want == key[0:1, c * 128 : (c + 1) * 128], 1.0, 0.0) for c in range(4)], axis=1
    ).astype(BF)
    fetches[1].wait()
    puts = []
    for k in range(K8):
        puts.append(pltpu.make_async_copy(features, out.at[k, pl.ds(32, 128), :], sems.at[4 + k]))
    for put in puts:
        put.start()
    fetches[2].wait()
    dense = jnp.dot(hot, bits[...].astype(F32).astype(BF), preferred_element_type=F32).astype(BF)
    for k in range(K8):
        words[k, :, 0:128] = dense[k * 64 : k * 64 + 32]
        words[k, :, 128:256] = dense[k * 64 + 32 : k * 64 + 64]
    last = pltpu.make_async_copy(words, out.at[:, pl.ds(0, 32), :], sems.at[20])
    last.start()
    for put in puts:
        put.wait()
    last.wait()


def unpacked(words):
    halves = []
    for h in range(2):
        half = words[:, h * 128 : (h + 1) * 128].astype(F32).astype(I32)
        spread = jnp.broadcast_to(half[:, None, :], (32, 8, 128))
        bits = jnp.bitwise_and(jnp.right_shift(spread, lax.broadcasted_iota(I32, (32, 8, 128), 1)), 1)
        halves.append(bits.reshape(256, 128).astype(F32).astype(BF))
    return jnp.concatenate(halves, axis=0)


def over_rows(block, source):
    return lax.dot_general(block, source, (((0,), (0,)), ((), ())), preferred_element_type=F32)


def forward_body(plane, out, own, turned):
    block = jnp.concatenate([unpacked(plane[k, 0:32, :]) for k in range(K8)], axis=1)
    source = plane[:, 32:160, :].reshape(K8 * 128, W)
    part = jnp.dot(block, source, preferred_element_type=F32)
    fourth = lax.broadcasted_iota(I32, (16, 1024), 1) // 256
    ones = jnp.where(fourth == lax.broadcasted_iota(I32, (16, 1024), 0), 1.0, 0.0).astype(BF)
    degree = lax.dot_general(ones, block, (((1,), (1,)), ((), ())), preferred_element_type=F32)
    for z in range(Z):
        mine = part[z * 32 : (z + 1) * 32]
        lanes = degree[0:8, (z // 4) * 128 : (z // 4 + 1) * 128]
        out[z] = jnp.concatenate([mine[:, 0:128], mine[:, 128:256], lanes], axis=0).astype(BF)
    x1, q, r = where_am_i()
    own[...] = plane[x1 * 4 + r, pl.ds(pl.multiple_of(32 + q * 32, 32), 32), :]
    turned[...] = block.T


def middle_body(parts, own, grads, weight, act, back, pushed, term):
    total = jnp.sum(parts[...].astype(F32), axis=0)
    degree = jnp.sum(total[64:68], axis=0, keepdims=True)
    first = (lax.axis_index("z") % 4) * 32
    pick = lax.broadcasted_iota(I32, (32, 128), 1) == lax.broadcasted_iota(I32, (32, 128), 0) + first
    counted = jnp.sum(jnp.where(pick, degree, 0.0), axis=1, keepdims=True)
    scaling = lax.rsqrt(1.0 + counted)
    gathered = jnp.concatenate([total[0:32], total[32:64]], axis=1)
    hidden = (own[...].astype(F32) + gathered * scaling).astype(BF)
    logits = jnp.dot(hidden, weight[...], preferred_element_type=F32)
    gate = jax.nn.sigmoid(logits)
    act[...] = (logits * gate).astype(BF)
    upstream = (grads[...].astype(F32) * gate * (1.0 + logits * (1.0 - gate))).astype(BF)
    hidden_grad = lax.dot_general(
        upstream, weight[...], (((1,), (1,)), ((), ())), preferred_element_type=F32
    )
    back[...] = hidden_grad
    pushed[...] = (hidden_grad * scaling).astype(BF)
    term[...] = over_rows(hidden, upstream).astype(BF)


def send_body(terms, pushed, out):
    extra = jnp.sum(terms[...].astype(F32), axis=0)
    message = jnp.concatenate([pushed[...].astype(F32), extra], axis=0).astype(BF)
    for z in range(Z):
        out[z] = message


def backward_body(turned, gathered, hidden_grad, out):
    x1, q, r = where_am_i()
    received = gathered[...]
    source = received[:, 0:32].reshape(Z * Q, W)
    extra = jnp.sum(received[:, 32:40].astype(F32), axis=0)
    own = hidden_grad[...]
    placed = jnp.concatenate([jnp.where(q == t, own, 0.0) for t in range(4)], axis=0)
    for k in range(K8):
        part = jnp.dot(turned[k * 128 : (k + 1) * 128, :], source, preferred_element_type=F32)
        part = part + jnp.where(x1 * 4 + r == k, placed, 0.0)
        out[k] = jnp.concatenate([part, extra], axis=0).astype(BF)


def share_body(parts, act, out):
    values = parts[...].astype(F32)
    out[0:128, :] = jnp.sum(values[:, 0:128], axis=0).astype(BF)
    out[128:192, :] = values[:, 128:136].reshape(64, W).astype(BF)
    out[192:224, :] = act[...]


def finish_body(shares, activation, weight_grad, input_grad):
    input_grad[...] = jnp.sum(shares[:, 0:128, :].astype(F32), axis=0).astype(BF)
    for r in range(R4):
        activation[r * 32 : (r + 1) * 32, :] = shares[r, 192:224, :]
        slices = shares[r, 128:192, :].astype(F32)
        for k in range(K8):
            weight_grad[k * 32 + r * 8 : k * 32 + r * 8 + 8, :] = slices[k * 8 : k * 8 + 8]


def per_device(features, weight, out_grad, tile_place, tile_bits, back_place, back_bits):
    near, far = pl.BlockSpec(memory_space=pltpu.VMEM), pl.BlockSpec(memory_space=pltpu.HBM)
    plane = pl.pallas_call(
        words_body,
        out_shape=jax.ShapeDtypeStruct((K8, 160, W), BF),
        in_specs=[far] * 3,
        out_specs=far,
        scratch_shapes=[
            pltpu.VMEM((1, 32), I32),
            pltpu.VMEM((512, 128), I32),
            pltpu.VMEM((128, W), BF),
            pltpu.VMEM((K8, 32, W), BF),
            pltpu.SemaphoreType.DMA((21,)),
        ],
        compiler_params=pltpu.CompilerParams(vmem_limit_bytes=FULL),
    )(back_place.reshape(1, 32), back_bits.reshape(512, 128), features)
    plane = lax.all_to_all(plane, ROWS2, 0, 0)
    _, _, r = where_am_i()
    grads = lax.ppermute(lax.dynamic_slice_in_dim(out_grad, r * Q, Q, 0), PLANE, swap_pairs())
    parts, own, turned = call(
        forward_body,
        (
            jax.ShapeDtypeStruct((Z, 72, 128), BF),
            jax.ShapeDtypeStruct((Q, W), BF),
            jax.ShapeDtypeStruct((K8 * 128, Z * Q), BF),
        ),
        plane,
    )
    parts = lax.all_to_all(parts, "z", 0, 0)
    act, hidden_grad, pushed, term = call(
        middle_body,
        (
            jax.ShapeDtypeStruct((Q, W), BF),
            jax.ShapeDtypeStruct((Q, W), F32),
            jax.ShapeDtypeStruct((Q, W), BF),
            jax.ShapeDtypeStruct((W, W), BF),
        ),
        parts,
        own,
        grads,
        weight,
    )
    act = lax.ppermute(act, PLANE, swap_pairs())
    terms = lax.all_to_all(term.reshape(PL, 8, W), PLANE, 0, 0)
    sent = call(send_body, jax.ShapeDtypeStruct((Z, 40, W), BF), terms, pushed)
    gathered = lax.all_to_all(sent, "z", 0, 0)
    parts = call(
        backward_body, jax.ShapeDtypeStruct((K8, 136, W), BF), turned, gathered, hidden_grad
    )
    parts = lax.all_to_all(parts, ROWS2, 0, 0)
    share = call(share_body, jax.ShapeDtypeStruct((224, W), BF), parts, act)
    shares = lax.all_gather(share, REP, axis=0)
    return call(
        finish_body,
        (
            jax.ShapeDtypeStruct((4 * Q, W), BF),
            jax.ShapeDtypeStruct((W, W), F32),
            jax.ShapeDtypeStruct((4 * Q, W), BF),
        ),
        shares,
    )


def solution(mesh):
    fine = Mesh(mesh.devices.reshape(16, 4, 2, 2, 2), ("z", "x", "yl", "yh", "c"))
    return jax.shard_map(
        per_device,
        mesh=fine,
        in_specs=(
            P(NODE, None),
            P(),
            P(NODE, None),
            P(NODE, REP, None),
            P(NODE, REP, None, None, None),
            P(NODE, REP, None),
            P(NODE, REP, None, None, None),
        ),
        out_specs=(P(NODE, None), P(), P(NODE, None)),
        check_vma=False,
    )
```

```python
import jax
import jax.numpy as jnp
from jax import lax
from jax.experimental import pallas as pl
from jax.experimental.pallas import tpu as pltpu
from jax.sharding import Mesh, PartitionSpec as P

BF, F32, I32 = jnp.bfloat16, jnp.float32, jnp.int32
NODE, REP = ("z", "x", "yl"), ("yh", "c")
ROWS2, PLANE = ("x", "yl"), ("x", "yl", "yh", "c")
Z, K8, R4, PL = 16, 8, 4, 32
Q, W = 32, 256
PARAMS = pltpu.CompilerParams(vmem_limit_bytes=24 * 1024 * 1024)


FULL = 62 * 1024 * 1024


def where_am_i():
    x = lax.axis_index("x")
    q = (x % 2) * 2 + lax.axis_index("yl")
    return x // 2, q, lax.axis_index("yh") * 2 + lax.axis_index("c")


def swap_pairs():
    pairs = []
    for x1 in range(2):
        for a in range(4):
            for b in range(4):
                pairs.append((x1 * 16 + a * 4 + b, x1 * 16 + b * 4 + a))
    return pairs


def call(body, shapes, *args):
    return pl.pallas_call(
        body,
        out_shape=shapes,
        in_specs=[pl.BlockSpec(memory_space=pltpu.VMEM)] * len(args),
        out_specs=jax.tree.map(lambda _: pl.BlockSpec(memory_space=pltpu.VMEM), shapes),
        compiler_params=PARAMS,
    )(*args)


def words_body(place_far, bits_far, features_far, out, place, bits, features, words, sems):
    fetches = [
        pltpu.make_async_copy(place_far, place, sems.at[0]),
        pltpu.make_async_copy(features_far, features, sems.at[1]),
        pltpu.make_async_copy(bits_far, bits, sems.at[3]),
    ]
    for fetch in fetches:
        fetch.start()
    row = lax.broadcasted_iota(I32, (512, 128), 0)
    want = (((row // 4) % 16) * 2 + row // 256) * 16 + ((row // 64) % 4) * 4 + row % 4
    lane = lax.broadcasted_iota(I32, (32, 512), 1)
    spread = jnp.where(lane // 16 == lax.broadcasted_iota(I32, (32, 512), 0), 1.0, 0.0).astype(BF)
    column = lax.broadcasted_iota(I32, (8, 512), 1) % 16
    fetches[0].wait()
    at = jnp.broadcast_to(place[...].astype(F32), (8, 32)).astype(BF)
    key = jnp.dot(at, spread, preferred_element_type=F32).astype(I32) * 16 + column
    hot = jnp.concatenate(
        [jnp.where(want == key[0:1, c * 128 : (c + 1) * 128], 1.0, 0.0) for c in range(4)], axis=1
    ).astype(BF)
    fetches[1].wait()
    puts = []
    for k in range(K8):
        puts.append(pltpu.make_async_copy(features, out.at[k, pl.ds(32, 128), :], sems.at[4 + k]))
    for put in puts:
        put.start()
    fetches[2].wait()
    dense = jnp.dot(hot, bits[...].astype(F32).astype(BF), preferred_element_type=F32).astype(BF)
    for k in range(K8):
        words[k, :, 0:128] = dense[k * 64 : k * 64 + 32]
        words[k, :, 128:256] = dense[k * 64 + 32 : k * 64 + 64]
    last = pltpu.make_async_copy(words, out.at[:, pl.ds(0, 32), :], sems.at[20])
    last.start()
    for put in puts:
        put.wait()
    last.wait()


def unpacked(words):
    halves = []
    for h in range(2):
        half = words[:, h * 128 : (h + 1) * 128].astype(F32).astype(I32)
        spread = jnp.broadcast_to(half[:, None, :], (32, 8, 128))
        bits = jnp.bitwise_and(jnp.right_shift(spread, lax.broadcasted_iota(I32, (32, 8, 128), 1)), 1)
        halves.append(bits.reshape(256, 128).astype(F32).astype(BF))
    return jnp.concatenate(halves, axis=0)


def over_rows(block, source):
    return lax.dot_general(block, source, (((0,), (0,)), ((), ())), preferred_element_type=F32)


def forward_body(plane, out, own, turned):
    block = jnp.concatenate([unpacked(plane[k, 0:32, :]) for k in range(K8)], axis=1)
    source = plane[:, 32:160, :].reshape(K8 * 128, W)
    part = jnp.dot(block, source, preferred_element_type=F32)
    fourth = lax.broadcasted_iota(I32, (16, 1024), 1) // 256
    ones = jnp.where(fourth == lax.broadcasted_iota(I32, (16, 1024), 0), 1.0, 0.0).astype(BF)
    degree = lax.dot_general(ones, block, (((1,), (1,)), ((), ())), preferred_element_type=F32)
    for z in range(Z):
        mine = part[z * 32 : (z + 1) * 32]
        lanes = degree[0:8, (z // 4) * 128 : (z // 4 + 1) * 128]
        out[z] = jnp.concatenate([mine[:, 0:128], mine[:, 128:256], lanes], axis=0).astype(BF)
    x1, q, r = where_am_i()
    own[...] = plane[x1 * 4 + r, pl.ds(pl.multiple_of(32 + q * 32, 32), 32), :]
    turned[...] = block.T


def middle_body(parts, own, grads, weight, act, back, pushed, term):
    total = jnp.sum(parts[...].astype(F32), axis=0)
    degree = jnp.sum(total[64:68], axis=0, keepdims=True)
    first = (lax.axis_index("z") % 4) * 32
    pick = lax.broadcasted_iota(I32, (32, 128), 1) == lax.broadcasted_iota(I32, (32, 128), 0) + first
    counted = jnp.sum(jnp.where(pick, degree, 0.0), axis=1, keepdims=True)
    scaling = lax.rsqrt(1.0 + counted)
    gathered = jnp.concatenate([total[0:32], total[32:64]], axis=1)
    hidden = (own[...].astype(F32) + gathered * scaling).astype(BF)
    logits = jnp.dot(hidden, weight[...], preferred_element_type=F32)
    gate = jax.nn.sigmoid(logits)
    act[...] = (logits * gate).astype(BF)
    upstream = (grads[...].astype(F32) * gate * (1.0 + logits * (1.0 - gate))).astype(BF)
    hidden_grad = lax.dot_general(
        upstream, weight[...], (((1,), (1,)), ((), ())), preferred_element_type=F32
    )
    back[...] = hidden_grad
    pushed[...] = (hidden_grad * scaling).astype(BF)
    term[...] = over_rows(hidden, upstream).astype(BF)


def send_body(terms, pushed, out):
    extra = jnp.sum(terms[...].astype(F32), axis=0)
    message = jnp.concatenate([pushed[...].astype(F32), extra], axis=0).astype(BF)
    for z in range(Z):
        out[z] = message


def backward_body(turned, gathered, hidden_grad, act, out, kept):
    kept[...] = act[...]
    x1, q, r = where_am_i()
    received = gathered[...]
    source = received[:, 0:32].reshape(Z * Q, W)
    extra = jnp.sum(received[:, 32:40].astype(F32), axis=0)
    own = hidden_grad[...]
    placed = jnp.concatenate([jnp.where(q == t, own, 0.0) for t in range(4)], axis=0)
    for k in range(K8):
        part = jnp.dot(turned[k * 128 : (k + 1) * 128, :], source, preferred_element_type=F32)
        part = part + jnp.where(x1 * 4 + r == k, placed, 0.0)
        out[k] = jnp.concatenate([part, extra], axis=0).astype(BF)


def share_body(parts, act, out):
    values = parts[...].astype(F32)
    out[0:128, :] = jnp.sum(values[:, 0:128], axis=0).astype(BF)
    out[128:192, :] = values[:, 128:136].reshape(64, W).astype(BF)
    out[192:224, :] = act[...]


def finish_body(shares, activation, weight_grad, input_grad):
    input_grad[...] = jnp.sum(shares[:, 0:128, :].astype(F32), axis=0).astype(BF)
    for r in range(R4):
        activation[r * 32 : (r + 1) * 32, :] = shares[r, 192:224, :]
        slices = shares[r, 128:192, :].astype(F32)
        for k in range(K8):
            weight_grad[k * 32 + r * 8 : k * 32 + r * 8 + 8, :] = slices[k * 8 : k * 8 + 8]


def per_device(features, weight, out_grad, tile_place, tile_bits, back_place, back_bits):
    near, far = pl.BlockSpec(memory_space=pltpu.VMEM), pl.BlockSpec(memory_space=pltpu.HBM)
    plane = pl.pallas_call(
        words_body,
        out_shape=jax.ShapeDtypeStruct((K8, 160, W), BF),
        in_specs=[far] * 3,
        out_specs=far,
        scratch_shapes=[
            pltpu.VMEM((1, 32), I32),
            pltpu.VMEM((512, 128), I32),
            pltpu.VMEM((128, W), BF),
            pltpu.VMEM((K8, 32, W), BF),
            pltpu.SemaphoreType.DMA((21,)),
        ],
        compiler_params=pltpu.CompilerParams(vmem_limit_bytes=FULL),
    )(back_place.reshape(1, 32), back_bits.reshape(512, 128), features)
    plane = lax.all_to_all(plane, ROWS2, 0, 0)
    _, _, r = where_am_i()
    grads = lax.ppermute(lax.dynamic_slice_in_dim(out_grad, r * Q, Q, 0), PLANE, swap_pairs())
    parts, own, turned = call(
        forward_body,
        (
            jax.ShapeDtypeStruct((Z, 72, 128), BF),
            jax.ShapeDtypeStruct((Q, W), BF),
            jax.ShapeDtypeStruct((K8 * 128, Z * Q), BF),
        ),
        plane,
    )
    parts = lax.all_to_all(parts, "z", 0, 0)
    act, hidden_grad, pushed, term = call(
        middle_body,
        (
            jax.ShapeDtypeStruct((Q, W), BF),
            jax.ShapeDtypeStruct((Q, W), F32),
            jax.ShapeDtypeStruct((Q, W), BF),
            jax.ShapeDtypeStruct((W, W), BF),
        ),
        parts,
        own,
        grads,
        weight,
    )
    act = lax.ppermute(act, PLANE, swap_pairs())
    terms = lax.all_to_all(term.reshape(PL, 8, W), PLANE, 0, 0)
    sent = call(send_body, jax.ShapeDtypeStruct((Z, 40, W), BF), terms, pushed)
    gathered = lax.all_to_all(sent, "z", 0, 0)
    parts, act = call(
        backward_body,
        (jax.ShapeDtypeStruct((K8, 136, W), BF), jax.ShapeDtypeStruct((Q, W), BF)),
        turned,
        gathered,
        hidden_grad,
        act,
    )
    parts = lax.all_to_all(parts, ROWS2, 0, 0)
    share = call(share_body, jax.ShapeDtypeStruct((224, W), BF), parts, act)
    shares = lax.all_gather(share, REP, axis=0)
    return call(
        finish_body,
        (
            jax.ShapeDtypeStruct((4 * Q, W), BF),
            jax.ShapeDtypeStruct((W, W), F32),
            jax.ShapeDtypeStruct((4 * Q, W), BF),
        ),
        shares,
    )


def solution(mesh):
    fine = Mesh(mesh.devices.reshape(16, 4, 2, 2, 2), ("z", "x", "yl", "yh", "c"))
    return jax.shard_map(
        per_device,
        mesh=fine,
        in_specs=(
            P(NODE, None),
            P(),
            P(NODE, None),
            P(NODE, REP, None),
            P(NODE, REP, None, None, None),
            P(NODE, REP, None),
            P(NODE, REP, None, None, None),
        ),
        out_specs=(P(NODE, None), P(), P(NODE, None)),
        check_vma=False,
    )
```
